256 devices in a mesh: dp: 128 (over y, z, x), tensor: 2 (over core).
Axes of the slice: x: 4, y: 4, z: 8, core: 2. Of those that a mesh axis runs over, the one named last changes fastest.
Arguments:
- gradients: bfloat16 [128, 3, 768, 768], P('dp', None, None, 'tensor'), may hold values from -60 to 60
- error_feedback: float32 [128, 3, 768, 768], P('dp', None, None, 'tensor'), may hold values from -4 to 4
- warm_start: float32 [3, 768, 32], replicated, may hold values from -0.21875 to 0.21875
- weights: bfloat16 [3, 768, 768], P(None, None, 'tensor'), may hold values from -4 to 4
Outputs:
- next_error: float32 [128, 3, 768, 768], P('dp', None, None, 'tensor')
- new_weights: bfloat16 [3, 768, 768], P(None, None, 'tensor')
- right_factor: float32 [3, 768, 32], replicated
The draws below stay inside these ranges and needn't reach their ends.
All inputs are finite; a program needn't handle non-finite values.
Results may differ from the reference program's by a relative error of at most 0.001.
Values sent between devices are 32-bit elements; how exact they have to be, the bound alone decides.
No kernel may reach another device: no remote copies, remote signals or barrier semaphores. Data moves between devices by JAX's collectives and lax.ppermute only.
A program may use at most 64 MiB of HBM per device.

```python
import math
import jax
import jax.numpy as jnp
from jax import lax

D = 768
ROWS = 768
MATS = 3
RANK = 32
REPLICAS = 128


def draw_gradients(key, part):
    key = jax.random.fold_in(key, 11)
    keys = jax.random.split(key, 3)
    shape = (REPLICAS, MATS, ROWS, D)
    row_scale = jnp.exp(jax.random.uniform(keys[0], (1, MATS, ROWS, 1), minval=math.log(0.5), maxval=math.log(2.0)))
    col_scale = jnp.exp(jax.random.uniform(keys[1], (1, MATS, 1, D), minval=math.log(0.3), maxval=math.log(3.0)))
    place = jnp.arange(REPLICAS, dtype=jnp.float32) / max(REPLICAS - 1, 1)
    replica_scale = jnp.exp(math.log(3.0) * place).reshape(REPLICAS, 1, 1, 1)
    base = jnp.clip(jax.random.normal(keys[2], shape), -4.0, 4.0)
    values = 0.5 * base * row_scale * col_scale * replica_scale
    return values.astype(jnp.bfloat16)


def shard_levels(key, dims, shards, least, high):
    factor_of = 1.0
    for dim, parts in shards:
        draws = jax.random.uniform(jax.random.fold_in(jax.random.fold_in(key, 6), dim), (parts,), jnp.float32, least / len(shards), high / len(shards))
        factor_of = factor_of * jnp.repeat(jnp.exp(draws), dims[dim] // parts).reshape((-1,) + (1,) * (len(dims) - 1 - dim))
    return factor_of


def scatter_about(key, dims, deviation, bound, shards=(), held_as=jnp.bfloat16):
    gain = shard_levels(key, dims, shards, -0.22, 0.18) if shards else 1.0
    result = jax.random.normal(key, dims, jnp.float32) * deviation * gain
    return jnp.minimum(jnp.maximum(result, -bound), bound).astype(held_as)


def setup_inputs(seed: int = 0) -> dict:
    seeds = jax.random.split(jax.random.key(seed), 5)
    gradients = draw_gradients(jax.random.fold_in(seeds[4], 71), 0)
    error_feedback = scatter_about(seeds[1], (REPLICAS, MATS, ROWS, D), 0.5, 4.0, ((0, 128), (3, 2)), jnp.float32)
    warm_start = scatter_about(seeds[2], (MATS, ROWS, RANK), ROWS ** -0.5, 0.21875, (), jnp.float32)
    weights = scatter_about(seeds[3], (MATS, ROWS, D), 0.25, 4.0, ((2, 2),))
    return {"gradients": gradients, "error_feedback": error_feedback, "warm_start": warm_start, "weights": weights}


def reference(gradients, error_feedback, warm_start, weights):
    exact = lax.Precision.HIGHEST
    merged = gradients.astype(jnp.float32) + error_feedback
    left = jnp.einsum('imrc,mrk->mck', merged, warm_start.astype(jnp.float32), precision=exact)
    gram = jnp.einsum('mck,mcl->mkl', left, left, precision=exact)
    lower = jnp.linalg.cholesky(gram)
    basis = lax.linalg.triangular_solve(lower, left, left_side=False, lower=True, transpose_a=True)
    right_factor = jnp.einsum('imrc,mck->mrk', merged, basis, precision=exact) / REPLICAS
    update = jnp.einsum('mrk,mck->mrc', right_factor, basis, precision=exact)
    next_error = merged - update[None]
    new_weights = (weights.astype(jnp.float32) - 0.5 * update).astype(jnp.bfloat16)
    return (next_error, new_weights, right_factor)
```

```python
import jax
import jax.numpy as jnp
from jax import lax
from jax.experimental import pallas as pl
from jax.experimental.pallas import tpu as pltpu
from jax.sharding import PartitionSpec as P

Y, PLANE = 4, 32
PLANES = [[y * PLANE + i for i in range(PLANE)] for y in range(Y)]
PAIR = [(0, 1), (1, 0)]
MATS, ROWS, HALF, RANK = 3, 768, 384, 32
EXACT = lax.Precision.HIGHEST
PARAMS = pltpu.CompilerParams(vmem_limit_bytes=24 * 1024 * 1024)
WHOLE = pl.BlockSpec(memory_space=pltpu.VMEM)


def split(x):
    high = x.astype(jnp.bfloat16)
    rest = x - high.astype(jnp.float32)
    mid = rest.astype(jnp.bfloat16)
    low = (rest - mid.astype(jnp.float32)).astype(jnp.bfloat16)
    return high, mid, low


def stacked_dot(small, large, axis):
    stack = jnp.concatenate(split(small), axis=0)
    total = None
    for part in split(large):
        term = lax.dot_general(
            stack, part, (((1,), (axis,)), ((), ())), preferred_element_type=jnp.float32
        )
        total = term if total is None else total + term
    return total[:RANK] + (total[RANK : 2 * RANK] + total[2 * RANK :])


def left_kernel(g_ref, e_ref, w_ref, left_ref, merged_ref):
    m = pl.program_id(0)
    merged = g_ref[...].astype(jnp.float32) + e_ref[...]
    merged_ref[m] = merged
    left = stacked_dot(w_ref[...].T, merged, 0)
    for i in range(MATS):

        @pl.when(m == i)
        def _():
            left_ref[:, i, :] = left


def local_left(gradients, error_feedback, warm_start):
    return pl.pallas_call(
        left_kernel,
        grid=(MATS,),
        in_specs=[
            pl.BlockSpec((None, None, ROWS, HALF), lambda m: (0, m, 0, 0)),
            pl.BlockSpec((None, None, ROWS, HALF), lambda m: (0, m, 0, 0)),
            pl.BlockSpec((None, ROWS, RANK), lambda m: (m, 0, 0)),
        ],
        out_specs=[
            pl.BlockSpec((RANK, MATS, HALF), lambda m: (0, 0, 0)),
            WHOLE,
        ],
        out_shape=[
            jax.ShapeDtypeStruct((RANK, MATS, HALF), jnp.float32),
            pltpu.VMEM((MATS, ROWS, HALF), jnp.float32),
        ],
        compiler_params=PARAMS,
        name="local_left",
    )(gradients, error_feedback, warm_start)


def right_kernel(core_ref, merged_ref, left_ref, own_ref, other_ref):
    first = core_ref[0] == 0
    for m in range(MATS):
        left = left_ref[:, m, :]
        right = stacked_dot(left, merged_ref[m], 1)
        low, high = right[:, :HALF], right[:, HALF:]
        own_ref[:, m, :] = jnp.where(first, low, high)
        other_ref[:, m, :HALF] = jnp.where(first, high, low)
        gram = lax.dot_general(
            left,
            left,
            (((1,), (1,)), ((), ())),
            precision=EXACT,
            preferred_element_type=jnp.float32,
        )
        other_ref[:, m, HALF:] = jnp.concatenate(
            [gram, jnp.zeros((RANK, 128 - RANK), jnp.float32)], axis=1
        )


def local_right(core, merged, left):
    return pl.pallas_call(
        right_kernel,
        in_specs=[pl.BlockSpec(memory_space=pltpu.SMEM), WHOLE, WHOLE],
        out_specs=[WHOLE, WHOLE],
        out_shape=[
            jax.ShapeDtypeStruct((RANK, MATS, HALF), jnp.float32),
            jax.ShapeDtypeStruct((RANK, MATS, HALF + 128), jnp.float32),
        ],
        compiler_params=PARAMS,
        name="local_right",
    )(core, merged, left)


def inverse_kernel(mine_ref, theirs_ref, inverse_ref):
    row = lax.broadcasted_iota(jnp.int32, (RANK, 2 * RANK), 0)
    lane = lax.broadcasted_iota(jnp.int32, (RANK, 2 * RANK), 1)
    one = (lane == row + RANK).astype(jnp.float32)[:, RANK:]
    tables, pivots = [], []
    for m in range(MATS):
        gram = mine_ref[:, m, HALF:] + theirs_ref[:, m, HALF:]
        tables.append(jnp.concatenate([gram[:, :RANK], one], axis=1))
        pivots.append(jnp.zeros((RANK, 1), jnp.float32))
    for j in range(RANK):
        for m in range(MATS):
            table = tables[m]
            pivot = table[j : j + 1, j : j + 1]
            factor = jnp.where(row[:, :1] > j, table[:, j : j + 1], 0.0) / pivot
            pivots[m] = jnp.where(row[:, :1] == j, pivot, pivots[m])
            tables[m] = table - factor * table[j : j + 1, :]
    for m in range(MATS):
        inverse_ref[m] = tables[m][:, RANK:] * lax.rsqrt(pivots[m])


def inverse_factor(mine, theirs):
    return pl.pallas_call(
        inverse_kernel,
        in_specs=[WHOLE, WHOLE],
        out_specs=WHOLE,
        out_shape=jax.ShapeDtypeStruct((MATS, RANK, RANK), jnp.float32),
        compiler_params=PARAMS,
        name="inverse_factor",
    )(mine, theirs)


def final_kernel(
    replicas,
    core_ref,
    merged_ref,
    left_ref,
    own_ref,
    other_ref,
    inverse_ref,
    weights_ref,
    error_ref,
    new_ref,
    right_ref,
):
    first = core_ref[0] == 0
    m = pl.program_id(0)
    for i in range(MATS):

        @pl.when(m == i)
        def _():
            own, other = own_ref[:, i, :], other_ref[:, i, :]
            total = jnp.concatenate(
                [jnp.where(first, own, other), jnp.where(first, other, own)], axis=1
            )
            inverse = inverse_ref[i]
            right = jnp.dot(
                inverse, total, precision=EXACT, preferred_element_type=jnp.float32
            ) * (1.0 / replicas)
            basis = jnp.dot(
                inverse,
                left_ref[:, i, :],
                precision=EXACT,
                preferred_element_type=jnp.float32,
            )
            right_ref[...] = right.T
            rh, rm, _ = split(right)
            bh, bm, _ = split(basis)
            update = lax.dot_general(
                jnp.concatenate([rh, rh, rm], axis=0),
                jnp.concatenate([bh, bm, bh], axis=0),
                (((0,), (0,)), ((), ())),
                preferred_element_type=jnp.float32,
            )
            error_ref[...] = merged_ref[i] - update
            weights = weights_ref[...].astype(jnp.float32)
            new_ref[...] = (weights - 0.5 * update).astype(jnp.bfloat16)


def finish(core, merged, left, own, other, inverse, weights, replicas):
    def kernel(*refs):
        final_kernel(replicas, *refs)

    return pl.pallas_call(
        kernel,
        grid=(MATS,),
        in_specs=[
            pl.BlockSpec(memory_space=pltpu.SMEM),
            WHOLE,
            WHOLE,
            WHOLE,
            WHOLE,
            WHOLE,
            pl.BlockSpec((None, ROWS, HALF), lambda m: (m, 0, 0)),
        ],
        out_specs=[
            pl.BlockSpec((None, None, ROWS, HALF), lambda m: (0, m, 0, 0)),
            pl.BlockSpec((None, ROWS, HALF), lambda m: (m, 0, 0)),
            pl.BlockSpec((None, ROWS, RANK), lambda m: (m, 0, 0)),
        ],
        out_shape=[
            jax.ShapeDtypeStruct((1, MATS, ROWS, HALF), jnp.float32),
            jax.ShapeDtypeStruct((MATS, ROWS, HALF), jnp.bfloat16),
            jax.ShapeDtypeStruct((MATS, ROWS, RANK), jnp.float32),
        ],
        compiler_params=PARAMS,
        name="finish",
    )(core, merged, left, own, other, inverse, weights)


def exchange(blocks):
    return lax.all_to_all(
        blocks, "dp", 0, 0, axis_index_groups=PLANES, tiled=True
    )


def sum_over_replicas(blocks):
    part = jnp.sum(exchange(blocks), axis=0)
    met = {}
    for step in (2, 1, 3):
        partners = [
            (y * PLANE + i, (y ^ step) * PLANE + i)
            for y in range(Y)
            for i in range(PLANE)
        ]
        met[step] = lax.ppermute(part, "dp", partners)
    total = (part + met[1]) + (met[2] + met[3])
    return exchange(jnp.broadcast_to(total[None], blocks.shape))


def body(gradients, error_feedback, warm_start, weights):
    replicas = lax.axis_size("dp")
    core = lax.axis_index("tensor").astype(jnp.int32)[None]
    with jax.named_scope("left"):
        blocks, merged = local_left(gradients, error_feedback, warm_start)
    with jax.named_scope("sum_left"):
        left = sum_over_replicas(blocks)
    with jax.named_scope("right"):
        own, other = local_right(core, merged, left)
        received = lax.ppermute(other, "tensor", PAIR)
        inverse = inverse_factor(other, received)
    with jax.named_scope("sum_right"):
        own = sum_over_replicas(own + received[:, :, :HALF])
        other = lax.ppermute(own, "tensor", PAIR)
    with jax.named_scope("finish"):
        next_error, new_weights, right_factor = finish(
            core, merged, left, own, other, inverse, weights, replicas
        )
    return (next_error, new_weights, right_factor)


def solution(mesh):
    return jax.shard_map(
        body,
        mesh=mesh,
        in_specs=(
            P("dp", None, None, "tensor"),
            P("dp", None, None, "tensor"),
            P(),
            P(None, None, "tensor"),
        ),
        out_specs=(P("dp", None, None, "tensor"), P(None, None, "tensor"), P()),
        check_vma=False,
    )
```

```python
import jax
import jax.numpy as jnp
from jax import lax
from jax.experimental import pallas as pl
from jax.experimental.pallas import tpu as pltpu
from jax.sharding import PartitionSpec as P

Y, PLANE = 4, 32
PLANES = [[y * PLANE + i for i in range(PLANE)] for y in range(Y)]
PAIR = [(0, 1), (1, 0)]
MATS, ROWS, HALF, RANK = 3, 768, 384, 32
EXACT = lax.Precision.HIGHEST
ORDER = (1, 2, 0)
CHUNK = 384
PARAMS = pltpu.CompilerParams(vmem_limit_bytes=24 * 1024 * 1024)
WHOLE = pl.BlockSpec(memory_space=pltpu.VMEM)


def in_hbm(x):
    return pltpu.with_memory_space_constraint(x, pltpu.HBM)


def split(x):
    high = x.astype(jnp.bfloat16)
    rest = x - high.astype(jnp.float32)
    mid = rest.astype(jnp.bfloat16)
    low = (rest - mid.astype(jnp.float32)).astype(jnp.bfloat16)
    return high, mid, low


def stacked_dot(small, large, axis):
    stack = jnp.concatenate(split(small), axis=0)
    total = None
    for part in split(large):
        term = lax.dot_general(
            stack, part, (((1,), (axis,)), ((), ())), preferred_element_type=jnp.float32
        )
        total = term if total is None else total + term
    return total[:RANK] + (total[RANK : 2 * RANK] + total[2 * RANK :])


def left_kernel(g_ref, e_ref, w_ref, left_ref, kept_ref, stored_ref, buffer, sem):
    m = pl.program_id(0)
    merged = g_ref[...].astype(jnp.float32) + e_ref[...]
    left = stacked_dot(w_ref[...], merged, 0)
    store = pltpu.make_async_copy(buffer, stored_ref, sem)
    for i in range(MATS):

        @pl.when(m == i)
        def _():
            left_ref[:, i, :] = left
            if i == 0:
                buffer[...] = merged
                store.start()
            else:
                kept_ref[i - 1] = merged
            if i == MATS - 1:
                store.wait()


def local_left(gradients, error_feedback, warm_rows):
    return pl.pallas_call(
        left_kernel,
        grid=(MATS,),
        in_specs=[
            pl.BlockSpec((None, None, ROWS, HALF), lambda m: (0, m, 0, 0)),
            pl.BlockSpec((None, None, ROWS, HALF), lambda m: (0, m, 0, 0)),
            pl.BlockSpec((None, RANK, ROWS), lambda m: (m, 0, 0)),
        ],
        out_specs=[
            pl.BlockSpec((RANK, MATS, HALF), lambda m: (0, 0, 0)),
            WHOLE,
            pl.BlockSpec(memory_space=pl.ANY),
        ],
        out_shape=[
            jax.ShapeDtypeStruct((RANK, MATS, HALF), jnp.float32),
            pltpu.VMEM((MATS - 1, ROWS, HALF), jnp.float32),
            pltpu.HBM((ROWS, HALF), jnp.float32),
        ],
        scratch_shapes=[
            pltpu.VMEM((ROWS, HALF), jnp.float32),
            pltpu.SemaphoreType.DMA,
        ],
        compiler_params=PARAMS,
        name="local_left",
    )(in_hbm(gradients), in_hbm(error_feedback), warm_rows)


def right_kernel(
    core_ref, kept_ref, stored_ref, left_ref, own_ref, other_ref, gram_ref, buffer, sem
):
    first = core_ref[0] == 0
    load = pltpu.make_async_copy(stored_ref, buffer, sem)
    load.start()
    for m in ORDER:
        left = left_ref[:, m, :]
        gram = lax.dot_general(
            left,
            left,
            (((1,), (1,)), ((), ())),
            precision=EXACT,
            preferred_element_type=jnp.float32,
        )
        gram = jnp.concatenate(
            [gram, jnp.zeros((RANK, 128 - RANK), jnp.float32)], axis=1
        )
        gram_ref[:, m, :] = gram
        other_ref[:, m, HALF:] = gram
        if m == 0:
            load.wait()
            merged = buffer[...]
        else:
            merged = kept_ref[m - 1]
        right = stacked_dot(left, merged, 1)
        low, high = right[:, :HALF], right[:, HALF:]
        own_ref[:, m, :] = jnp.where(first, low, high)
        other_ref[:, m, :HALF] = jnp.where(first, high, low)


def local_right(core, kept, stored, left):
    return pl.pallas_call(
        right_kernel,
        in_specs=[
            pl.BlockSpec(memory_space=pltpu.SMEM),
            WHOLE,
            pl.BlockSpec(memory_space=pl.ANY),
            WHOLE,
        ],
        out_specs=[WHOLE] * 3,
        out_shape=[
            jax.ShapeDtypeStruct((RANK, MATS, HALF), jnp.float32),
            jax.ShapeDtypeStruct((RANK, MATS, HALF + 128), jnp.float32),
            jax.ShapeDtypeStruct((RANK, MATS, 128), jnp.float32),
        ],
        scratch_shapes=[
            pltpu.VMEM((ROWS, HALF), jnp.float32),
            pltpu.SemaphoreType.DMA,
        ],
        compiler_params=PARAMS,
        name="local_right",
    )(core, kept, in_hbm(stored), left)


def inverse_kernel(gram_ref, inverse_ref):
    row = lax.broadcasted_iota(jnp.int32, (RANK, 2 * RANK), 0)
    lane = lax.broadcasted_iota(jnp.int32, (RANK, 2 * RANK), 1)
    one = (lane == row + RANK).astype(jnp.float32)[:, RANK:]
    tables, pivots = [], []
    for m in range(MATS):
        tables.append(jnp.concatenate([gram_ref[:, m, :RANK], one], axis=1))
        pivots.append(jnp.zeros((RANK, 1), jnp.float32))
    for j in range(RANK):
        for m in range(MATS):
            table = tables[m]
            pivot = table[j : j + 1, j : j + 1]
            factor = jnp.where(row[:, :1] > j, table[:, j : j + 1], 0.0) / pivot
            pivots[m] = jnp.where(row[:, :1] == j, pivot, pivots[m])
            tables[m] = table - factor * table[j : j + 1, :]
    for m in range(MATS):
        inverse_ref[m] = tables[m][:, RANK:] * lax.rsqrt(pivots[m])


def inverse_factor(gram):
    return pl.pallas_call(
        inverse_kernel,
        in_specs=[WHOLE],
        out_specs=WHOLE,
        out_shape=jax.ShapeDtypeStruct((MATS, RANK, RANK), jnp.float32),
        compiler_params=PARAMS,
        cost_estimate=pl.CostEstimate(
            flops=4_000_000, bytes_accessed=100_000, transcendentals=0
        ),
        name="inverse_factor",
    )(gram)


def finish_kernel(
    replicas,
    core_ref,
    kept_ref,
    stored_ref,
    left_ref,
    own_ref,
    other_ref,
    inverse_ref,
    weights_ref,
    error_ref,
    new_ref,
    right_ref,
    buffer,
    right_parts,
    basis_parts,
    sem,
):
    first = core_ref[0] == 0
    p, c = pl.program_id(0), pl.program_id(1)
    load = pltpu.make_async_copy(stored_ref, buffer, sem)
    rows = pl.ds(pl.multiple_of(c * CHUNK, CHUNK), CHUNK)

    @pl.when((p == 0) & (c == 0))
    def _():
        load.start()

    for i, m in enumerate(ORDER):

        @pl.when((p == i) & (c == 0))
        def _():
            own, other = own_ref[:, m, :], other_ref[:, m, :]
            total = jnp.concatenate(
                [jnp.where(first, own, other), jnp.where(first, other, own)], axis=1
            )
            inverse = inverse_ref[m]
            right = jnp.dot(
                inverse, total, precision=EXACT, preferred_element_type=jnp.float32
            ) * (1.0 / replicas)
            basis = jnp.dot(
                inverse,
                left_ref[:, m, :],
                precision=EXACT,
                preferred_element_type=jnp.float32,
            )
            right_ref[...] = right
            high, mid, _ = split(right)
            right_parts[...] = jnp.concatenate([high, high, mid], axis=0)
            high, mid, _ = split(basis)
            basis_parts[...] = jnp.concatenate([high, mid, high], axis=0)
            if m == 0:
                load.wait()

    update = lax.dot_general(
        right_parts[:, rows],
        basis_parts[...],
        (((0,), (0,)), ((), ())),
        preferred_element_type=jnp.float32,
    )
    weights = weights_ref[...].astype(jnp.float32)
    new_ref[...] = (weights - 0.5 * update).astype(jnp.bfloat16)
    for i, m in enumerate(ORDER):

        @pl.when(p == i)
        def _():
            merged = buffer[rows, :] if m == 0 else kept_ref[m - 1, rows, :]
            error_ref[...] = merged - update


def finish(core, kept, stored, left, own, other, inverse, weights, replicas):
    def kernel(*refs):
        finish_kernel(replicas, *refs)

    def at(p, c):
        return (lax.rem(p + 1, MATS), c, 0)

    return pl.pallas_call(
        kernel,
        grid=(MATS, ROWS // CHUNK),
        in_specs=[
            pl.BlockSpec(memory_space=pltpu.SMEM),
            WHOLE,
            pl.BlockSpec(memory_space=pl.ANY),
            WHOLE,
            WHOLE,
            WHOLE,
            WHOLE,
            pl.BlockSpec((None, CHUNK, HALF), at),
        ],
        out_specs=[
            pl.BlockSpec((None, None, CHUNK, HALF), lambda p, c: (0, *at(p, c))),
            pl.BlockSpec((None, CHUNK, HALF), at),
            pl.BlockSpec((None, RANK, ROWS), lambda p, c: (at(p, c)[0], 0, 0)),
        ],
        out_shape=[
            jax.ShapeDtypeStruct((1, MATS, ROWS, HALF), jnp.float32),
            jax.ShapeDtypeStruct((MATS, ROWS, HALF), jnp.bfloat16),
            jax.ShapeDtypeStruct((MATS, RANK, ROWS), jnp.float32),
        ],
        scratch_shapes=[
            pltpu.VMEM((ROWS, HALF), jnp.float32),
            pltpu.VMEM((3 * RANK, ROWS), jnp.bfloat16),
            pltpu.VMEM((3 * RANK, HALF), jnp.bfloat16),
            pltpu.SemaphoreType.DMA,
        ],
        compiler_params=PARAMS,
        name="finish",
    )(core, kept, in_hbm(stored), left, own, other, inverse, in_hbm(weights))


def exchange(blocks):
    return lax.all_to_all(
        blocks, "dp", 0, 0, axis_index_groups=PLANES, tiled=True
    )


def sum_over_replicas(blocks, beside=None):
    part = jnp.sum(exchange(blocks), axis=0)
    result = None
    if beside is not None:
        work, value = beside
        part, value = lax.optimization_barrier((part, value))
    met = {}
    for step in (2, 1, 3):
        partners = [
            (y * PLANE + i, (y ^ step) * PLANE + i)
            for y in range(Y)
            for i in range(PLANE)
        ]
        met[step] = lax.ppermute(part, "dp", partners)
    if beside is not None:
        result = work(value)
        met[1], met[2], met[3], result = lax.optimization_barrier(
            (met[1], met[2], met[3], result)
        )
    total = (part + met[1]) + (met[2] + met[3])
    return exchange(jnp.broadcast_to(total[None], blocks.shape)), result


def body(gradients, error_feedback, warm_start, weights):
    replicas = lax.axis_size("dp")
    core = lax.axis_index("tensor").astype(jnp.int32)[None]
    with jax.named_scope("left"):
        blocks, kept, stored = local_left(
            gradients, error_feedback, jnp.swapaxes(warm_start, 1, 2)
        )
    with jax.named_scope("sum_left"):
        left, _ = sum_over_replicas(blocks)
    with jax.named_scope("right"):
        own, other, gram = local_right(core, kept, stored, left)
        received = lax.ppermute(other, "tensor", PAIR)
        gram = gram + received[:, :, HALF:]
    with jax.named_scope("sum_right"):
        own, inverse = sum_over_replicas(
            own + received[:, :, :HALF], (inverse_factor, gram)
        )
        other = lax.ppermute(own, "tensor", PAIR)
    with jax.named_scope("finish"):
        next_error, new_weights, right_rows = finish(
            core, kept, stored, left, own, other, inverse, weights, replicas
        )
    return (next_error, new_weights, jnp.swapaxes(right_rows, 1, 2))


def solution(mesh):
    return jax.shard_map(
        body,
        mesh=mesh,
        in_specs=(
            P("dp", None, None, "tensor"),
            P("dp", None, None, "tensor"),
            P(),
            P(None, None, "tensor"),
        ),
        out_specs=(P("dp", None, None, "tensor"), P(None, None, "tensor"), P()),
        check_vma=False,
    )
```

```python
import jax
import jax.numpy as jnp
from jax import lax
from jax.experimental import pallas as pl
from jax.experimental.pallas import tpu as pltpu
from jax.sharding import PartitionSpec as P

Y, PLANE = 4, 32
PLANES = [[y * PLANE + i for i in range(PLANE)] for y in range(Y)]
PAIR = [(0, 1), (1, 0)]
MATS, ROWS, HALF, RANK = 3, 768, 384, 32
EXACT = lax.Precision.HIGHEST
KEPT = 2
ORDER = tuple(range(MATS))
CHUNK = 384
PARAMS = pltpu.CompilerParams(vmem_limit_bytes=24 * 1024 * 1024)
PARTS_LEFT = 2
PARTS_RIGHT = 2
ANYWHERE = pl.BlockSpec(memory_space=pl.ANY)
WHOLE = pl.BlockSpec(memory_space=pltpu.VMEM)


def in_hbm(x):
    return pltpu.with_memory_space_constraint(x, pltpu.HBM)


def split(x):
    high = x.astype(jnp.bfloat16)
    rest = x - high.astype(jnp.float32)
    mid = rest.astype(jnp.bfloat16)
    low = (rest - mid.astype(jnp.float32)).astype(jnp.bfloat16)
    return high, mid, low


def streamed_dot(left, merged):
    stack = jnp.concatenate(split(left), axis=0)
    flat = merged.T
    result = None
    for part in split(flat)[:PARTS_RIGHT]:
        term = jnp.dot(stack, part, preferred_element_type=jnp.float32)
        result = term if result is None else result + term
    return result[:RANK] + (result[RANK : 2 * RANK] + result[2 * RANK : 3 * RANK])


def fetches(g_ref, e_ref, g_buf, e_refs, sems, m):
    return (
        pltpu.make_async_copy(g_ref.at[0, m], g_buf, sems.at[m, 0]),
        pltpu.make_async_copy(e_ref.at[0, m], e_refs, sems.at[m, 1]),
    )


def left_kernel(g_ref, e_ref, w_ref, left_ref, kept_ref, g_buf, e_buf, w_buf, sems, w_sem):
    w_copy = pltpu.make_async_copy(w_ref, w_buf, w_sem)
    w_copy.start()
    held = [kept_ref.at[m] if m < KEPT else e_buf.at[m - KEPT] for m in range(MATS)]
    copies = [
        fetches(g_ref, e_ref, g_buf.at[m], held[m], sems, m) for m in range(MATS)
    ]
    for pair in copies:
        for copy in pair:
            copy.start()
    w_copy.wait()
    for m in range(MATS):
        stack = jnp.concatenate(split(w_buf[m]), axis=0)
        for copy in copies[m]:
            copy.wait()
        merged = g_buf[m].astype(jnp.float32) + held[m][...]
        if m < KEPT:
            kept_ref[m] = merged
        total = None
        for part in split(merged)[:PARTS_LEFT]:
            term = jnp.dot(stack, part, preferred_element_type=jnp.float32)
            total = term if total is None else total + term
        left_ref[:, m, :] = total[:RANK] + (total[RANK : 2 * RANK] + total[2 * RANK :])


def local_left(gradients, error_feedback, warm_rows):
    return pl.pallas_call(
        left_kernel,
        in_specs=[ANYWHERE] * 3,
        out_specs=[WHOLE, WHOLE],
        out_shape=[
            jax.ShapeDtypeStruct((RANK, MATS, HALF), jnp.float32),
            pltpu.VMEM((KEPT, ROWS, HALF), jnp.float32),
        ],
        scratch_shapes=[
            pltpu.VMEM((MATS, ROWS, HALF), jnp.bfloat16),
            pltpu.VMEM((MATS - KEPT, ROWS, HALF), jnp.float32),
            pltpu.VMEM((MATS, RANK, ROWS), jnp.float32),
            pltpu.SemaphoreType.DMA((MATS, 2)),
            pltpu.SemaphoreType.DMA,
        ],
        compiler_params=PARAMS,
        name="local_left",
    )(in_hbm(gradients), in_hbm(error_feedback), in_hbm(warm_rows))


def right_kernel(
    core_ref, kept_ref, g_ref, e_ref, left_ref, own_ref, other_ref, gram_ref, g_buf, e_buf, sems
):
    first = core_ref[0] == 0
    copies = {
        m: fetches(g_ref, e_ref, g_buf.at[m - KEPT], e_buf.at[m - KEPT], sems, m)
        for m in range(KEPT, MATS)
    }
    for pair in copies.values():
        for copy in pair:
            copy.start()
    for m in range(MATS):
        left = left_ref[:, m, :]
        gram = lax.dot_general(
            left,
            left,
            (((1,), (1,)), ((), ())),
            precision=EXACT,
            preferred_element_type=jnp.float32,
        )
        gram = jnp.concatenate(
            [gram, jnp.zeros((RANK, 128 - RANK), jnp.float32)], axis=1
        )
        gram_ref[:, m, :] = gram
        other_ref[:, m, HALF:] = gram
        if m < KEPT:
            merged = kept_ref[m]
        else:
            for copy in copies[m]:
                copy.wait()
            merged = g_buf[m - KEPT].astype(jnp.float32) + e_buf[m - KEPT]
        right = streamed_dot(left, merged)
        low, high = right[:, :HALF], right[:, HALF:]
        own_ref[:, m, :] = jnp.where(first, low, high)
        other_ref[:, m, :HALF] = jnp.where(first, high, low)


def local_right(core, kept, gradients, error_feedback, left):
    return pl.pallas_call(
        right_kernel,
        in_specs=[
            pl.BlockSpec(memory_space=pltpu.SMEM),
            WHOLE,
            ANYWHERE,
            ANYWHERE,
            WHOLE,
        ],
        out_specs=[WHOLE] * 3,
        out_shape=[
            jax.ShapeDtypeStruct((RANK, MATS, HALF), jnp.float32),
            jax.ShapeDtypeStruct((RANK, MATS, HALF + 128), jnp.float32),
            jax.ShapeDtypeStruct((RANK, MATS, 128), jnp.float32),
        ],
        scratch_shapes=[
            pltpu.VMEM((MATS - KEPT, ROWS, HALF), jnp.bfloat16),
            pltpu.VMEM((MATS - KEPT, ROWS, HALF), jnp.float32),
            pltpu.SemaphoreType.DMA((MATS, 2)),
        ],
        compiler_params=PARAMS,
        name="local_right",
    )(core, kept, in_hbm(gradients), in_hbm(error_feedback), left)


def inverse_kernel(gram_ref, inverse_ref):
    row = lax.broadcasted_iota(jnp.int32, (RANK, 2 * RANK), 0)
    lane = lax.broadcasted_iota(jnp.int32, (RANK, 2 * RANK), 1)
    one = (lane == row + RANK).astype(jnp.float32)[:, RANK:]
    tables, pivots = [], []
    for m in range(MATS):
        tables.append(jnp.concatenate([gram_ref[:, m, :RANK], one], axis=1))
        pivots.append(jnp.zeros((RANK, 1), jnp.float32))
    for j in range(RANK):
        for m in range(MATS):
            table = tables[m]
            pivot = table[j : j + 1, j : j + 1]
            factor = jnp.where(row[:, :1] > j, table[:, j : j + 1], 0.0) / pivot
            pivots[m] = jnp.where(row[:, :1] == j, pivot, pivots[m])
            tables[m] = table - factor * table[j : j + 1, :]
    for m in range(MATS):
        inverse_ref[m] = tables[m][:, RANK:] * lax.rsqrt(pivots[m])


def inverse_factor(gram):
    return pl.pallas_call(
        inverse_kernel,
        in_specs=[WHOLE],
        out_specs=WHOLE,
        out_shape=jax.ShapeDtypeStruct((MATS, RANK, RANK), jnp.float32),
        compiler_params=PARAMS,
        cost_estimate=pl.CostEstimate(
            flops=4_000_000, bytes_accessed=100_000, transcendentals=0
        ),
        name="inverse_factor",
    )(gram)


def finish_kernel(
    replicas,
    core_ref,
    kept_ref,
    g_ref,
    e_ref,
    left_ref,
    own_ref,
    other_ref,
    inverse_ref,
    weights_ref,
    error_ref,
    new_ref,
    right_ref,
    g_buf,
    m_buf,
    w_buf,
    e_buf,
    r_buf,
    in_sems,
    w_sems,
    out_sems,
):
    first = core_ref[0] == 0
    loads = []
    for m in range(MATS):
        pair = ()
        if m >= KEPT:
            pair = fetches(
                g_ref, e_ref, g_buf.at[m - KEPT], m_buf.at[m - KEPT], in_sems, m
            )
        loads.append(
            (pltpu.make_async_copy(weights_ref.at[m], w_buf.at[m], w_sems.at[m]), *pair)
        )
    for group in loads:
        for copy in group:
            copy.start()
    stores = []

    def store(source, target):
        copy = pltpu.make_async_copy(source, target, out_sems.at[len(stores)])
        copy.start()
        stores.append(copy)

    for m in ORDER:
        own, other = own_ref[:, m, :], other_ref[:, m, :]
        total = jnp.concatenate(
            [jnp.where(first, own, other), jnp.where(first, other, own)], axis=1
        )
        inverse = inverse_ref[m]
        right = jnp.dot(
            inverse, total, precision=EXACT, preferred_element_type=jnp.float32
        ) * (1.0 / replicas)
        basis = jnp.dot(
            inverse,
            left_ref[:, m, :],
            precision=EXACT,
            preferred_element_type=jnp.float32,
        )
        r_buf[m] = right
        store(r_buf.at[m], right_ref.at[m])
        high, mid, _ = split(right)
        rights = jnp.concatenate([high, high, mid], axis=0)
        high, mid, _ = split(basis)
        bases = jnp.concatenate([high, mid, high], axis=0)
        for copy in loads[m]:
            copy.wait()
        for c in range(ROWS // CHUNK):
            rows = pl.ds(c * CHUNK, CHUNK)
            update = lax.dot_general(
                rights[:, c * CHUNK : (c + 1) * CHUNK],
                bases,
                (((0,), (0,)), ((), ())),
                preferred_element_type=jnp.float32,
            )
            if m < KEPT:
                merged = kept_ref[m, rows, :]
            else:
                merged = g_buf[m - KEPT, rows, :].astype(jnp.float32)
                merged = merged + m_buf[m - KEPT, rows, :]
            e_buf[m, rows, :] = merged - update
            store(e_buf.at[m, rows], error_ref.at[0, m, rows])
            weights = w_buf[m, rows, :].astype(jnp.float32)
            w_buf[m, rows, :] = (weights - 0.5 * update).astype(jnp.bfloat16)
            store(w_buf.at[m, rows], new_ref.at[m, rows])
    for copy in stores:
        copy.wait()


def finish(
    core, kept, gradients, error_feedback, left, own, other, inverse, weights, replicas
):
    def kernel(*refs):
        finish_kernel(replicas, *refs)

    return pl.pallas_call(
        kernel,
        in_specs=[
            pl.BlockSpec(memory_space=pltpu.SMEM),
            WHOLE,
            ANYWHERE,
            ANYWHERE,
            WHOLE,
            WHOLE,
            WHOLE,
            WHOLE,
            ANYWHERE,
        ],
        out_specs=[ANYWHERE] * 3,
        out_shape=[
            pltpu.HBM((1, MATS, ROWS, HALF), jnp.float32),
            pltpu.HBM((MATS, ROWS, HALF), jnp.bfloat16),
            pltpu.HBM((MATS, RANK, ROWS), jnp.float32),
        ],
        scratch_shapes=[
            pltpu.VMEM((MATS - KEPT, ROWS, HALF), jnp.bfloat16),
            pltpu.VMEM((MATS - KEPT, ROWS, HALF), jnp.float32),
            pltpu.VMEM((MATS, ROWS, HALF), jnp.bfloat16),
            pltpu.VMEM((MATS, ROWS, HALF), jnp.float32),
            pltpu.VMEM((MATS, RANK, ROWS), jnp.float32),
            pltpu.SemaphoreType.DMA((MATS, 2)),
            pltpu.SemaphoreType.DMA((MATS,)),
            pltpu.SemaphoreType.DMA((MATS * (1 + 2 * ROWS // CHUNK),)),
        ],
        compiler_params=PARAMS,
        name="finish",
    )(
        core,
        kept,
        in_hbm(gradients),
        in_hbm(error_feedback),
        left,
        own,
        other,
        inverse,
        in_hbm(weights),
    )


def exchange(blocks):
    return lax.all_to_all(
        blocks, "dp", 0, 0, axis_index_groups=PLANES, tiled=True
    )


def sum_over_replicas(blocks, beside=None):
    part = jnp.sum(exchange(blocks), axis=0)
    result = None
    if beside is not None:
        work, value = beside
        part, value = lax.optimization_barrier((part, value))
    met = {}
    for step in (2, 1, 3):
        partners = [
            (y * PLANE + i, (y ^ step) * PLANE + i)
            for y in range(Y)
            for i in range(PLANE)
        ]
        met[step] = lax.ppermute(part, "dp", partners)
    if beside is not None:
        result = work(value)
        met[1], met[2], met[3], result = lax.optimization_barrier(
            (met[1], met[2], met[3], result)
        )
    total = (part + met[1]) + (met[2] + met[3])
    return exchange(jnp.broadcast_to(total[None], blocks.shape)), result


def body(gradients, error_feedback, warm_start, weights):
    replicas = lax.axis_size("dp")
    core = lax.axis_index("tensor").astype(jnp.int32)[None]
    with jax.named_scope("left"):
        blocks, kept = local_left(
            gradients, error_feedback, jnp.swapaxes(warm_start, 1, 2)
        )
    with jax.named_scope("sum_left"):
        blocks, core = lax.optimization_barrier((blocks, core))
        left, _ = sum_over_replicas(blocks)
    with jax.named_scope("right"):
        own, other, gram = local_right(core, kept, gradients, error_feedback, left)
        received = lax.ppermute(other, "tensor", PAIR)
        own, gram = lax.optimization_barrier(
            (own + received[:, :, :HALF], gram + received[:, :, HALF:])
        )
    with jax.named_scope("sum_right"):
        own, inverse = sum_over_replicas(own, (inverse_factor, gram))
        other = lax.ppermute(own, "tensor", PAIR)
    with jax.named_scope("finish"):
        next_error, new_weights, right_rows = finish(
            core,
            kept,
            gradients,
            error_feedback,
            left,
            own,
            other,
            inverse,
            weights,
            replicas,
        )
    return (next_error, new_weights, jnp.swapaxes(right_rows, 1, 2))


def solution(mesh):
    return jax.shard_map(
        body,
        mesh=mesh,
        in_specs=(
            P("dp", None, None, "tensor"),
            P("dp", None, None, "tensor"),
            P(),
            P(None, None, "tensor"),
        ),
        out_specs=(P("dp", None, None, "tensor"), P(None, None, "tensor"), P()),
        check_vma=False,
    )
```

```python
import jax
import jax.numpy as jnp
from jax import lax
from jax.experimental import pallas as pl
from jax.experimental.pallas import tpu as pltpu
from jax.sharding import PartitionSpec as P

Y, Z, X = 4, 8, 4
BLOCKS = 32
LAYERS = [
    [(y * Z + z) * X + x for z in pair for y in range(Y) for x in range(X)]
    for pair in ((0, 1), (3, 2), (4, 5), (7, 6))
]
MEETINGS = ((7, 2, 1, 4, 3, 6, 5, 0), (3, 6, 5, 0, 7, 2, 1, 4), (4, 5, 6, 7, 0, 1, 2, 3))
PAIR = [(0, 1), (1, 0)]
MATS, ROWS, HALF, RANK = 3, 768, 384, 32
EXACT = lax.Precision.HIGHEST
KEPT = 2
ORDER = tuple(range(MATS))
CHUNK = 384
PARAMS = pltpu.CompilerParams(vmem_limit_bytes=24 * 1024 * 1024)
PARTS_LEFT = 2
PARTS_RIGHT = 2
ANYWHERE = pl.BlockSpec(memory_space=pl.ANY)
WHOLE = pl.BlockSpec(memory_space=pltpu.VMEM)


def in_hbm(x):
    return pltpu.with_memory_space_constraint(x, pltpu.HBM)


def split(x):
    high = x.astype(jnp.bfloat16)
    rest = x - high.astype(jnp.float32)
    mid = rest.astype(jnp.bfloat16)
    low = (rest - mid.astype(jnp.float32)).astype(jnp.bfloat16)
    return high, mid, low


def streamed_dot(left, merged):
    stack = jnp.concatenate(split(left), axis=0)
    result = jnp.dot(
        jnp.concatenate([stack] * PARTS_RIGHT, axis=1),
        jnp.concatenate(split(merged.T)[:PARTS_RIGHT], axis=0),
        preferred_element_type=jnp.float32,
    )
    return result[:RANK] + (result[RANK : 2 * RANK] + result[2 * RANK :])


def fetches(g_ref, e_ref, g_buf, e_refs, sems, m):
    return (
        pltpu.make_async_copy(g_ref.at[0, m], g_buf, sems.at[m, 0]),
        pltpu.make_async_copy(e_ref.at[0, m], e_refs, sems.at[m, 1]),
    )


def left_kernel(g_ref, e_ref, w_ref, left_ref, kept_ref, g_buf, e_buf, w_buf, sems, w_sem):
    w_copy = pltpu.make_async_copy(w_ref, w_buf, w_sem)
    w_copy.start()
    held = [kept_ref.at[m] if m < KEPT else e_buf.at[m - KEPT] for m in range(MATS)]
    copies = [
        fetches(g_ref, e_ref, g_buf.at[m], held[m], sems, m) for m in range(MATS)
    ]
    for pair in copies:
        for copy in pair:
            copy.start()
    w_copy.wait()
    for m in range(MATS):
        stack = jnp.concatenate(split(w_buf[m]), axis=0)
        for copy in copies[m]:
            copy.wait()
        merged = g_buf[m].astype(jnp.float32) + held[m][...]
        if m < KEPT:
            kept_ref[m] = merged
        total = jnp.dot(
            jnp.concatenate([stack] * PARTS_LEFT, axis=1),
            jnp.concatenate(split(merged)[:PARTS_LEFT], axis=0),
            preferred_element_type=jnp.float32,
        )
        left_ref[:, m, :] = total[:RANK] + (total[RANK : 2 * RANK] + total[2 * RANK :])


def local_left(gradients, error_feedback, warm_rows):
    return pl.pallas_call(
        left_kernel,
        in_specs=[ANYWHERE] * 3,
        out_specs=[WHOLE, WHOLE],
        out_shape=[
            jax.ShapeDtypeStruct((RANK, MATS, HALF), jnp.float32),
            pltpu.VMEM((KEPT, ROWS, HALF), jnp.float32),
        ],
        scratch_shapes=[
            pltpu.VMEM((MATS, ROWS, HALF), jnp.bfloat16),
            pltpu.VMEM((MATS - KEPT, ROWS, HALF), jnp.float32),
            pltpu.VMEM((MATS, RANK, ROWS), jnp.float32),
            pltpu.SemaphoreType.DMA((MATS, 2)),
            pltpu.SemaphoreType.DMA,
        ],
        compiler_params=PARAMS,
        name="local_left",
    )(in_hbm(gradients), in_hbm(error_feedback), in_hbm(warm_rows))


def right_kernel(own, *refs):
    core_ref, kept_ref, g_ref, e_ref, left_ref, out_ref = refs[:6]
    g_buf, e_buf, sems = refs[-3:]
    core = core_ref[0]
    start = (core if own else 1 - core) * HALF
    rows = pl.ds(pl.multiple_of(start, HALF), HALF)
    copies = {}
    for m in range(KEPT, MATS):
        copies[m] = (
            pltpu.make_async_copy(g_ref.at[0, m, rows], g_buf.at[m - KEPT], sems.at[m, 0]),
            pltpu.make_async_copy(e_ref.at[0, m, rows], e_buf.at[m - KEPT], sems.at[m, 1]),
        )
        for copy in copies[m]:
            copy.start()
    for m in range(MATS):
        left = left_ref[:, m, :]
        if not own:
            gram = lax.dot_general(
                left,
                left,
                (((1,), (1,)), ((), ())),
                precision=EXACT,
                preferred_element_type=jnp.float32,
            )
            gram = jnp.concatenate(
                [gram, jnp.zeros((RANK, 128 - RANK), jnp.float32)], axis=1
            )
            refs[6][:, m, :] = gram
            out_ref[:, m, HALF:] = gram
        if m < KEPT:
            merged = kept_ref[m, rows, :]
        else:
            for copy in copies[m]:
                copy.wait()
            merged = g_buf[m - KEPT].astype(jnp.float32) + e_buf[m - KEPT]
        out_ref[:, m, :HALF] = streamed_dot(left, merged)


def local_right(own, core, kept, gradients, error_feedback, left):
    def kernel(*refs):
        right_kernel(own, *refs)

    half = jax.ShapeDtypeStruct((RANK, MATS, HALF), jnp.float32)
    pair = [
        jax.ShapeDtypeStruct((RANK, MATS, HALF + 128), jnp.float32),
        jax.ShapeDtypeStruct((RANK, MATS, 128), jnp.float32),
    ]
    return pl.pallas_call(
        kernel,
        in_specs=[
            pl.BlockSpec(memory_space=pltpu.SMEM),
            WHOLE,
            ANYWHERE,
            ANYWHERE,
            WHOLE,
        ],
        out_specs=WHOLE if own else [WHOLE] * 2,
        out_shape=half if own else pair,
        scratch_shapes=[
            pltpu.VMEM((MATS - KEPT, HALF, HALF), jnp.bfloat16),
            pltpu.VMEM((MATS - KEPT, HALF, HALF), jnp.float32),
            pltpu.SemaphoreType.DMA((MATS, 2)),
        ],
        compiler_params=PARAMS,
        cost_estimate=pl.CostEstimate(
            flops=200_000_000, bytes_accessed=2_000_000, transcendentals=0
        ),
        name="right_own" if own else "right_other",
    )(core, kept, in_hbm(gradients), in_hbm(error_feedback), left)


def inverse_kernel(gram_ref, inverse_ref):
    group, blocks = 4, RANK // 8
    wide = (8, 2 * RANK)
    row = lax.broadcasted_iota(jnp.int32, (RANK, RANK), 0)
    lane = lax.broadcasted_iota(jnp.int32, (RANK, RANK), 1)
    one = (lane == row).astype(jnp.float32)
    below = lax.broadcasted_iota(jnp.int32, wide, 0)
    tables, pivots = [], []
    for m in range(MATS):
        table = jnp.concatenate([gram_ref[:, m, :RANK], one], axis=1)
        tables.append([table[8 * b : 8 * b + 8] for b in range(blocks)])
        pivots.append([jnp.zeros(wide, jnp.float32)] * blocks)
    for j in range(0, RANK, group):
        home, at = j // 8, j % 8
        live = range(home, blocks)
        for m in range(MATS):
            table = tables[m]
            columns = [
                {b: jnp.broadcast_to(table[b][:, j + q : j + q + 1], wide) for b in live}
                for q in range(group)
            ]
            rows = [table[home][at + q : at + q + 1] for q in range(group)]
            for q in range(group):
                pivot = columns[q][home][at + q : at + q + 1]
                pivots[m][home] = jnp.where(below == at + q, pivot, pivots[m][home])
                over = 1.0 / pivot
                scaled = rows[q] * over
                factor = dict(columns[q])
                factor[home] = jnp.where(below > at + q, factor[home], 0.0)
                for later in range(q + 1, group):
                    ratio = columns[later][home][at + q : at + q + 1] * over
                    for b in live:
                        columns[later][b] = columns[later][b] - factor[b] * ratio
                    rows[later] = (
                        rows[later] - factor[home][at + later : at + later + 1] * scaled
                    )
                for b in live:
                    table[b] = table[b] - factor[b] * scaled
    for m in range(MATS):
        table = jnp.concatenate([block[:, RANK:] for block in tables[m]], axis=0)
        pivot = jnp.concatenate([block[:, RANK:] for block in pivots[m]], axis=0)
        inverse_ref[m] = table * lax.rsqrt(pivot)


def inverse_factor(gram):
    return pl.pallas_call(
        inverse_kernel,
        in_specs=[WHOLE],
        out_specs=WHOLE,
        out_shape=jax.ShapeDtypeStruct((MATS, RANK, RANK), jnp.float32),
        compiler_params=PARAMS,
        cost_estimate=pl.CostEstimate(
            flops=4_000_000, bytes_accessed=100_000, transcendentals=0
        ),
        name="inverse_factor",
    )(gram)


def finish_kernel(
    replicas,
    core_ref,
    kept_ref,
    g_ref,
    e_ref,
    left_ref,
    own_ref,
    other_ref,
    inverse_ref,
    weights_ref,
    error_ref,
    new_ref,
    right_ref,
    g_buf,
    m_buf,
    w_buf,
    e_buf,
    r_buf,
    in_sems,
    w_sems,
    out_sems,
):
    first = core_ref[0] == 0
    loads = []
    for m in range(MATS):
        pair = ()
        if m >= KEPT:
            pair = fetches(
                g_ref, e_ref, g_buf.at[m - KEPT], m_buf.at[m - KEPT], in_sems, m
            )
        loads.append(
            (pltpu.make_async_copy(weights_ref.at[m], w_buf.at[m], w_sems.at[m]), *pair)
        )
    for group in loads:
        for copy in group:
            copy.start()
    stores = []

    def store(source, target):
        copy = pltpu.make_async_copy(source, target, out_sems.at[len(stores)])
        copy.start()
        stores.append(copy)

    for m in ORDER:
        own, other = own_ref[:, m, :], other_ref[:, m, :]
        total = jnp.concatenate(
            [jnp.where(first, own, other), jnp.where(first, other, own)], axis=1
        )
        inverse = inverse_ref[m]
        right = jnp.dot(
            inverse, total, precision=EXACT, preferred_element_type=jnp.float32
        ) * (1.0 / replicas)
        basis = jnp.dot(
            inverse,
            left_ref[:, m, :],
            precision=EXACT,
            preferred_element_type=jnp.float32,
        )
        r_buf[m] = right
        store(r_buf.at[m], right_ref.at[m])
        high, mid, _ = split(right)
        rights = jnp.concatenate([high, high, mid], axis=0)
        high, mid, _ = split(basis)
        bases = jnp.concatenate([high, mid, high], axis=0)
        for copy in loads[m]:
            copy.wait()
        for c in range(ROWS // CHUNK):
            rows = pl.ds(c * CHUNK, CHUNK)
            update = lax.dot_general(
                rights[:, c * CHUNK : (c + 1) * CHUNK],
                bases,
                (((0,), (0,)), ((), ())),
                preferred_element_type=jnp.float32,
            )
            if m < KEPT:
                merged = kept_ref[m, rows, :]
            else:
                merged = g_buf[m - KEPT, rows, :].astype(jnp.float32)
                merged = merged + m_buf[m - KEPT, rows, :]
            e_buf[m, rows, :] = merged - update
            store(e_buf.at[m, rows], error_ref.at[0, m, rows])
            weights = w_buf[m, rows, :].astype(jnp.float32)
            w_buf[m, rows, :] = (weights - 0.5 * update).astype(jnp.bfloat16)
            store(w_buf.at[m, rows], new_ref.at[m, rows])
    for copy in stores:
        copy.wait()


def finish(
    core, kept, gradients, error_feedback, left, own, other, inverse, weights, replicas
):
    def kernel(*refs):
        finish_kernel(replicas, *refs)

    return pl.pallas_call(
        kernel,
        in_specs=[
            pl.BlockSpec(memory_space=pltpu.SMEM),
            WHOLE,
            ANYWHERE,
            ANYWHERE,
            WHOLE,
            WHOLE,
            WHOLE,
            WHOLE,
            ANYWHERE,
        ],
        out_specs=[ANYWHERE] * 3,
        out_shape=[
            pltpu.HBM((1, MATS, ROWS, HALF), jnp.float32),
            pltpu.HBM((MATS, ROWS, HALF), jnp.bfloat16),
            pltpu.HBM((MATS, RANK, ROWS), jnp.float32),
        ],
        scratch_shapes=[
            pltpu.VMEM((MATS - KEPT, ROWS, HALF), jnp.bfloat16),
            pltpu.VMEM((MATS - KEPT, ROWS, HALF), jnp.float32),
            pltpu.VMEM((MATS, ROWS, HALF), jnp.bfloat16),
            pltpu.VMEM((MATS, ROWS, HALF), jnp.float32),
            pltpu.VMEM((MATS, RANK, ROWS), jnp.float32),
            pltpu.SemaphoreType.DMA((MATS, 2)),
            pltpu.SemaphoreType.DMA((MATS,)),
            pltpu.SemaphoreType.DMA((MATS * (1 + 2 * ROWS // CHUNK),)),
        ],
        compiler_params=PARAMS,
        name="finish",
    )(
        core,
        kept,
        in_hbm(gradients),
        in_hbm(error_feedback),
        left,
        own,
        other,
        inverse,
        in_hbm(weights),
    )


def exchange(blocks):
    return lax.all_to_all(blocks, "dp", 0, 0, axis_index_groups=LAYERS, tiled=True)


def sum_over_replicas(blocks, beside=None):
    part = jnp.sum(exchange(blocks), axis=0)
    result = None
    if beside is not None:
        work, value = beside
        part, value = lax.optimization_barrier((part, value))
    met = []
    for meeting in MEETINGS:
        partners = [
            ((y * Z + z) * X + x, (y * Z + meeting[z]) * X + x)
            for y in range(Y)
            for z in range(Z)
            for x in range(X)
        ]
        met.append(lax.ppermute(part, "dp", partners))
    if beside is not None:
        result = work(value)
        *met, result = lax.optimization_barrier((*met, result))
    total = (part + met[0]) + (met[1] + met[2])
    return exchange(jnp.broadcast_to(total[None], blocks.shape)), result


def body(gradients, error_feedback, warm_start, weights):
    replicas = lax.axis_size("dp")
    core = lax.axis_index("tensor").astype(jnp.int32)[None]
    with jax.named_scope("left"):
        blocks, kept = local_left(
            gradients, error_feedback, jnp.swapaxes(warm_start, 1, 2)
        )
    with jax.named_scope("sum_left"):
        blocks, core = lax.optimization_barrier((blocks, core))
        left, _ = sum_over_replicas(blocks)
    with jax.named_scope("right"):
        other, gram = local_right(False, core, kept, gradients, error_feedback, left)
        received = lax.ppermute(other, "tensor", PAIR)
        own = local_right(True, core, kept, gradients, error_feedback, left)
        own, gram = lax.optimization_barrier(
            (own + received[:, :, :HALF], gram + received[:, :, HALF:])
        )
    with jax.named_scope("sum_right"):
        own, inverse = sum_over_replicas(own, (inverse_factor, gram))
        other = lax.ppermute(own, "tensor", PAIR)
    with jax.named_scope("finish"):
        next_error, new_weights, right_rows = finish(
            core,
            kept,
            gradients,
            error_feedback,
            left,
            own,
            other,
            inverse,
            weights,
            replicas,
        )
    return (next_error, new_weights, jnp.swapaxes(right_rows, 1, 2))


def solution(mesh):
    return jax.shard_map(
        body,
        mesh=mesh,
        in_specs=(
            P("dp", None, None, "tensor"),
            P("dp", None, None, "tensor"),
            P(),
            P(None, None, "tensor"),
        ),
        out_specs=(P("dp", None, None, "tensor"), P(None, None, "tensor"), P()),
        check_vma=False,
    )
```

```python
import jax
import jax.numpy as jnp
from jax import lax
from jax.experimental import pallas as pl
from jax.experimental.pallas import tpu as pltpu
from jax.sharding import PartitionSpec as P

Y, Z, X = 4, 8, 4
BLOCKS = 32
LAYERS = [
    [(y * Z + z) * X + x for z in pair for y in range(Y) for x in range(X)]
    for pair in ((0, 1), (3, 2), (4, 5), (7, 6))
]
MEETINGS = ((7, 2, 1, 4, 3, 6, 5, 0), (3, 6, 5, 0, 7, 2, 1, 4), (4, 5, 6, 7, 0, 1, 2, 3))
PAIR = [(0, 1), (1, 0)]
MATS, ROWS, HALF, RANK = 3, 768, 384, 32
WIDTH = MATS * HALF
EXACT = lax.Precision.HIGHEST
KEPT = 2
ORDER = tuple(range(MATS))
CHUNK = 384
PARAMS = pltpu.CompilerParams(vmem_limit_bytes=24 * 1024 * 1024)
PARTS_LEFT = 2
PARTS_RIGHT = 2
ANYWHERE = pl.BlockSpec(memory_space=pl.ANY)
WHOLE = pl.BlockSpec(memory_space=pltpu.VMEM)


def at(m):
    return slice(m * HALF, (m + 1) * HALF)


def in_hbm(x):
    return pltpu.with_memory_space_constraint(x, pltpu.HBM)


def split(x):
    high = x.astype(jnp.bfloat16)
    rest = x - high.astype(jnp.float32)
    mid = rest.astype(jnp.bfloat16)
    low = (rest - mid.astype(jnp.float32)).astype(jnp.bfloat16)
    return high, mid, low


def streamed_dot(left, merged):
    high, mid, low = split(left.T)
    stack = jnp.concatenate([high, mid, low, jnp.zeros_like(low)], axis=1)
    result = jnp.dot(
        jnp.concatenate(split(merged)[:PARTS_RIGHT], axis=1),
        jnp.concatenate([stack] * PARTS_RIGHT, axis=0),
        preferred_element_type=jnp.float32,
    ).T
    return result[:RANK] + (result[RANK : 2 * RANK] + result[2 * RANK : 3 * RANK])


def turned_dot(left, merged):
    stack = jnp.concatenate(split(left), axis=0)
    result = jnp.dot(
        jnp.concatenate([stack] * PARTS_RIGHT, axis=1),
        jnp.concatenate(split(merged.T)[:PARTS_RIGHT], axis=0),
        preferred_element_type=jnp.float32,
    )
    return result[:RANK] + (result[RANK : 2 * RANK] + result[2 * RANK :])


def fetches(g_ref, e_ref, g_buf, e_refs, sems, m):
    return (
        pltpu.make_async_copy(g_ref.at[0, m], g_buf, sems.at[m, 0]),
        pltpu.make_async_copy(e_ref.at[0, m], e_refs, sems.at[m, 1]),
    )


def half_of(core, own):
    return pl.ds(pl.multiple_of((core if own else 1 - core) * HALF, HALF), HALF)


def left_kernel(
    core_ref, g_ref, e_ref, w_ref, left_ref, kept_ref, half_ref, g_buf, e_buf, w_buf, sems, w_sem
):
    w_copy = pltpu.make_async_copy(w_ref, w_buf, w_sem)
    w_copy.start()
    held = [kept_ref.at[m] if m < KEPT else e_buf.at[m - KEPT] for m in range(MATS)]
    copies = [
        fetches(g_ref, e_ref, g_buf.at[m], held[m], sems, m) for m in range(MATS)
    ]
    for pair in copies:
        for copy in pair:
            copy.start()
    w_copy.wait()
    for m in range(MATS):
        stack = jnp.concatenate(split(w_buf[m]), axis=0)
        for copy in copies[m]:
            copy.wait()
        merged = g_buf[m].astype(jnp.float32) + held[m][...]
        if m < KEPT:
            kept_ref[m] = merged
        else:
            first = core_ref[0] == 0
            half_ref[m - KEPT] = jnp.where(first, merged[HALF:], merged[:HALF])
        total = jnp.dot(
            jnp.concatenate([stack] * PARTS_LEFT, axis=1),
            jnp.concatenate(split(merged)[:PARTS_LEFT], axis=0),
            preferred_element_type=jnp.float32,
        )
        left_ref[:, 0, at(m)] = total[:RANK] + (total[RANK : 2 * RANK] + total[2 * RANK :])


def local_left(core, gradients, error_feedback, warm_rows):
    return pl.pallas_call(
        left_kernel,
        in_specs=[pl.BlockSpec(memory_space=pltpu.SMEM)] + [ANYWHERE] * 3,
        out_specs=[WHOLE] * 3,
        out_shape=[
            pltpu.VMEM((RANK, 1, WIDTH), jnp.float32),
            pltpu.VMEM((KEPT, ROWS, HALF), jnp.float32),
            pltpu.VMEM((MATS - KEPT, HALF, HALF), jnp.float32),
        ],
        scratch_shapes=[
            pltpu.VMEM((MATS, ROWS, HALF), jnp.bfloat16),
            pltpu.VMEM((MATS - KEPT, ROWS, HALF), jnp.float32),
            pltpu.VMEM((MATS, RANK, ROWS), jnp.float32),
            pltpu.SemaphoreType.DMA((MATS, 2)),
            pltpu.SemaphoreType.DMA,
        ],
        compiler_params=PARAMS,
        name="local_left",
    )(core, in_hbm(gradients), in_hbm(error_feedback), in_hbm(warm_rows))


def right_other_kernel(core_ref, kept_ref, half_ref, left_ref, out_ref, gram_ref):
    rows = half_of(core_ref[0], False)
    for m in range(MATS):
        left = left_ref[:, 0, at(m)]
        gram = lax.dot_general(
            left,
            left,
            (((1,), (1,)), ((), ())),
            precision=EXACT,
            preferred_element_type=jnp.float32,
        )
        gram = jnp.concatenate(
            [gram, jnp.zeros((RANK, 128 - RANK), jnp.float32)], axis=1
        )
        gram_ref[:, 0, m * 128 : (m + 1) * 128] = gram
        out_ref[:, 0, WIDTH + m * 128 : WIDTH + (m + 1) * 128] = gram
        merged = kept_ref[m, rows, :] if m < KEPT else half_ref[m - KEPT]
        out_ref[:, 0, at(m)] = streamed_dot(left, merged)


def right_own_kernel(
    core_ref, kept_ref, g_ref, e_ref, left_ref, out_ref, g_buf, e_buf, sems
):
    rows = half_of(core_ref[0], True)
    copies = {}
    for m in range(KEPT, MATS):
        copies[m] = (
            pltpu.make_async_copy(g_ref.at[0, m, rows], g_buf.at[m - KEPT], sems.at[m, 0]),
            pltpu.make_async_copy(e_ref.at[0, m, rows], e_buf.at[m - KEPT], sems.at[m, 1]),
        )
        for copy in copies[m]:
            copy.start()
    for m in range(MATS):
        if m < KEPT:
            merged = kept_ref[m, rows, :]
        else:
            for copy in copies[m]:
                copy.wait()
            merged = g_buf[m - KEPT].astype(jnp.float32) + e_buf[m - KEPT]
        out_ref[:, 0, at(m)] = turned_dot(left_ref[:, 0, at(m)], merged)


def right_other(core, kept, half, left):
    return pl.pallas_call(
        right_other_kernel,
        in_specs=[pl.BlockSpec(memory_space=pltpu.SMEM)] + [WHOLE] * 3,
        out_specs=[WHOLE] * 2,
        out_shape=[
            pltpu.VMEM((RANK, 1, WIDTH + MATS * 128), jnp.float32),
            pltpu.VMEM((RANK, 1, MATS * 128), jnp.float32),
        ],
        compiler_params=PARAMS,
        name="right_other",
    )(core, kept, half, left)


def right_own(core, kept, gradients, error_feedback, left):
    return pl.pallas_call(
        right_own_kernel,
        in_specs=[
            pl.BlockSpec(memory_space=pltpu.SMEM),
            WHOLE,
            ANYWHERE,
            ANYWHERE,
            WHOLE,
        ],
        out_specs=WHOLE,
        out_shape=pltpu.VMEM((RANK, 1, WIDTH), jnp.float32),
        scratch_shapes=[
            pltpu.VMEM((MATS - KEPT, HALF, HALF), jnp.bfloat16),
            pltpu.VMEM((MATS - KEPT, HALF, HALF), jnp.float32),
            pltpu.SemaphoreType.DMA((MATS, 2)),
        ],
        compiler_params=PARAMS,
        cost_estimate=pl.CostEstimate(
            flops=200_000_000, bytes_accessed=2_000_000, transcendentals=0
        ),
        name="right_own",
    )(core, kept, in_hbm(gradients), in_hbm(error_feedback), left)


def inverse_kernel(gram_ref, inverse_ref):
    group, blocks = 4, RANK // 8
    wide = (8, 2 * RANK)
    row = lax.broadcasted_iota(jnp.int32, (RANK, RANK), 0)
    lane = lax.broadcasted_iota(jnp.int32, (RANK, RANK), 1)
    one = (lane == row).astype(jnp.float32)
    below = lax.broadcasted_iota(jnp.int32, wide, 0)
    tables, pivots = [], []
    for m in range(MATS):
        table = jnp.concatenate([gram_ref[:, 0, m * 128 : m * 128 + RANK], one], axis=1)
        tables.append([table[8 * b : 8 * b + 8] for b in range(blocks)])
        pivots.append([jnp.zeros(wide, jnp.float32)] * blocks)
    for j in range(0, RANK, group):
        home, at = j // 8, j % 8
        live = range(home, blocks)
        for m in range(MATS):
            table = tables[m]
            columns = [
                {b: jnp.broadcast_to(table[b][:, j + q : j + q + 1], wide) for b in live}
                for q in range(group)
            ]
            rows = [table[home][at + q : at + q + 1] for q in range(group)]
            for q in range(group):
                pivot = columns[q][home][at + q : at + q + 1]
                pivots[m][home] = jnp.where(below == at + q, pivot, pivots[m][home])
                over = 1.0 / pivot
                scaled = rows[q] * over
                factor = dict(columns[q])
                factor[home] = jnp.where(below > at + q, factor[home], 0.0)
                for later in range(q + 1, group):
                    ratio = columns[later][home][at + q : at + q + 1] * over
                    for b in live:
                        columns[later][b] = columns[later][b] - factor[b] * ratio
                    rows[later] = (
                        rows[later] - factor[home][at + later : at + later + 1] * scaled
                    )
                for b in live:
                    table[b] = table[b] - factor[b] * scaled
    for m in range(MATS):
        table = jnp.concatenate([block[:, RANK:] for block in tables[m]], axis=0)
        pivot = jnp.concatenate([block[:, RANK:] for block in pivots[m]], axis=0)
        inverse_ref[m] = table * lax.rsqrt(pivot)


def inverse_factor(gram):
    return pl.pallas_call(
        inverse_kernel,
        in_specs=[WHOLE],
        out_specs=WHOLE,
        out_shape=jax.ShapeDtypeStruct((MATS, RANK, RANK), jnp.float32),
        compiler_params=PARAMS,
        cost_estimate=pl.CostEstimate(
            flops=4_000_000, bytes_accessed=100_000, transcendentals=0
        ),
        name="inverse_factor",
    )(gram)


def finish_kernel(
    replicas,
    core_ref,
    kept_ref,
    g_ref,
    e_ref,
    left_ref,
    own_ref,
    other_ref,
    inverse_ref,
    weights_ref,
    error_ref,
    new_ref,
    right_ref,
    g_buf,
    m_buf,
    w_buf,
    e_buf,
    r_buf,
    in_sems,
    w_sems,
    out_sems,
):
    first = core_ref[0] == 0
    loads = []
    for m in range(MATS):
        pair = ()
        if m >= KEPT:
            pair = fetches(
                g_ref, e_ref, g_buf.at[m - KEPT], m_buf.at[m - KEPT], in_sems, m
            )
        loads.append(
            (pltpu.make_async_copy(weights_ref.at[m], w_buf.at[m], w_sems.at[m]), *pair)
        )
    for group in loads:
        for copy in group:
            copy.start()
    stores = []

    def store(source, target):
        copy = pltpu.make_async_copy(source, target, out_sems.at[len(stores)])
        copy.start()
        stores.append(copy)

    for m in ORDER:
        own, other = own_ref[:, 0, at(m)], other_ref[:, 0, at(m)]
        total = jnp.concatenate(
            [jnp.where(first, own, other), jnp.where(first, other, own)], axis=1
        )
        inverse = inverse_ref[m]
        right = jnp.dot(
            inverse, total, precision=EXACT, preferred_element_type=jnp.float32
        ) * (1.0 / replicas)
        basis = jnp.dot(
            inverse,
            left_ref[:, 0, at(m)],
            precision=EXACT,
            preferred_element_type=jnp.float32,
        )
        r_buf[m] = right
        store(r_buf.at[m], right_ref.at[m])
        high, mid, _ = split(right)
        rights = jnp.concatenate([high, high, mid], axis=0)
        high, mid, _ = split(basis)
        bases = jnp.concatenate([high, mid, high], axis=0)
        for copy in loads[m]:
            copy.wait()
        for c in range(ROWS // CHUNK):
            rows = pl.ds(c * CHUNK, CHUNK)
            update = lax.dot_general(
                rights[:, c * CHUNK : (c + 1) * CHUNK],
                bases,
                (((0,), (0,)), ((), ())),
                preferred_element_type=jnp.float32,
            )
            if m < KEPT:
                merged = kept_ref[m, rows, :]
            else:
                merged = g_buf[m - KEPT, rows, :].astype(jnp.float32)
                merged = merged + m_buf[m - KEPT, rows, :]
            e_buf[m, rows, :] = merged - update
            store(e_buf.at[m, rows], error_ref.at[0, m, rows])
            weights = w_buf[m, rows, :].astype(jnp.float32)
            w_buf[m, rows, :] = (weights - 0.5 * update).astype(jnp.bfloat16)
            store(w_buf.at[m, rows], new_ref.at[m, rows])
    for copy in stores:
        copy.wait()


def finish(
    core, kept, gradients, error_feedback, left, own, other, inverse, weights, replicas
):
    def kernel(*refs):
        finish_kernel(replicas, *refs)

    return pl.pallas_call(
        kernel,
        in_specs=[
            pl.BlockSpec(memory_space=pltpu.SMEM),
            WHOLE,
            ANYWHERE,
            ANYWHERE,
            WHOLE,
            WHOLE,
            WHOLE,
            WHOLE,
            ANYWHERE,
        ],
        out_specs=[ANYWHERE] * 3,
        out_shape=[
            pltpu.HBM((1, MATS, ROWS, HALF), jnp.float32),
            pltpu.HBM((MATS, ROWS, HALF), jnp.bfloat16),
            pltpu.HBM((MATS, RANK, ROWS), jnp.float32),
        ],
        scratch_shapes=[
            pltpu.VMEM((MATS - KEPT, ROWS, HALF), jnp.bfloat16),
            pltpu.VMEM((MATS - KEPT, ROWS, HALF), jnp.float32),
            pltpu.VMEM((MATS, ROWS, HALF), jnp.bfloat16),
            pltpu.VMEM((MATS, ROWS, HALF), jnp.float32),
            pltpu.VMEM((MATS, RANK, ROWS), jnp.float32),
            pltpu.SemaphoreType.DMA((MATS, 2)),
            pltpu.SemaphoreType.DMA((MATS,)),
            pltpu.SemaphoreType.DMA((MATS * (1 + 2 * ROWS // CHUNK),)),
        ],
        compiler_params=PARAMS,
        name="finish",
    )(
        core,
        kept,
        in_hbm(gradients),
        in_hbm(error_feedback),
        left,
        own,
        other,
        inverse,
        in_hbm(weights),
    )


def exchange(blocks):
    return lax.all_to_all(blocks, "dp", 0, 0, axis_index_groups=LAYERS, tiled=True)


def sum_over_replicas(blocks, beside=None):
    part = jnp.sum(exchange(blocks), axis=0)
    result = None
    if beside is not None:
        work, value = beside
        part, value = lax.optimization_barrier((part, value))
    met = []
    for meeting in MEETINGS:
        partners = [
            ((y * Z + z) * X + x, (y * Z + meeting[z]) * X + x)
            for y in range(Y)
            for z in range(Z)
            for x in range(X)
        ]
        met.append(lax.ppermute(part, "dp", partners))
    if beside is not None:
        result = work(value)
        *met, result = lax.optimization_barrier((*met, result))
    total = (part + met[0]) + (met[1] + met[2])
    return exchange(jnp.broadcast_to(total[None], blocks.shape)), result


def body(gradients, error_feedback, warm_start, weights):
    replicas = lax.axis_size("dp")
    core = lax.axis_index("tensor").astype(jnp.int32)[None]
    with jax.named_scope("left"):
        blocks, kept, half = local_left(
            core, gradients, error_feedback, jnp.swapaxes(warm_start, 1, 2)
        )
    with jax.named_scope("sum_left"):
        blocks, core = lax.optimization_barrier((blocks, core))
        left, _ = sum_over_replicas(blocks)
    with jax.named_scope("right"):
        other, gram = right_other(core, kept, half, left)
        received = lax.ppermute(other, "tensor", PAIR)
        own = right_own(core, kept, gradients, error_feedback, left)
        own, gram = lax.optimization_barrier(
            (own + received[:, :, :WIDTH], gram + received[:, :, WIDTH:])
        )
    with jax.named_scope("sum_right"):
        own, inverse = sum_over_replicas(own, (inverse_factor, gram))
        other = lax.ppermute(own, "tensor", PAIR)
    with jax.named_scope("finish"):
        next_error, new_weights, right_rows = finish(
            core,
            kept,
            gradients,
            error_feedback,
            left,
            own,
            other,
            inverse,
            weights,
            replicas,
        )
    return (next_error, new_weights, jnp.swapaxes(right_rows, 1, 2))


def solution(mesh):
    return jax.shard_map(
        body,
        mesh=mesh,
        in_specs=(
            P("dp", None, None, "tensor"),
            P("dp", None, None, "tensor"),
            P(),
            P(None, None, "tensor"),
        ),
        out_specs=(P("dp", None, None, "tensor"), P(None, None, "tensor"), P()),
        check_vma=False,
    )
```

```python
import jax
import jax.numpy as jnp
from jax import lax
from jax.experimental import pallas as pl
from jax.experimental.pallas import tpu as pltpu
from jax.sharding import PartitionSpec as P

Y, Z, X = 4, 8, 4
BLOCKS = 32
LAYERS = [
    [(y * Z + z) * X + x for z in pair for y in range(Y) for x in range(X)]
    for pair in ((0, 1), (3, 2), (4, 5), (7, 6))
]
MEETINGS = ((7, 2, 1, 4, 3, 6, 5, 0), (3, 6, 5, 0, 7, 2, 1, 4), (4, 5, 6, 7, 0, 1, 2, 3))
PAIR = [(0, 1), (1, 0)]
MATS, ROWS, HALF, RANK = 3, 768, 384, 32
WIDTH = MATS * HALF
EXACT = lax.Precision.HIGHEST
KEPT = 2
ORDER = tuple(range(MATS))
CHUNK = 384
PARAMS = pltpu.CompilerParams(vmem_limit_bytes=24 * 1024 * 1024)
PARTS_LEFT = 2
PARTS_RIGHT = 2
ANYWHERE = pl.BlockSpec(memory_space=pl.ANY)
WHOLE = pl.BlockSpec(memory_space=pltpu.VMEM)


def at(m):
    return slice(m * HALF, (m + 1) * HALF)


def in_hbm(x):
    return pltpu.with_memory_space_constraint(x, pltpu.HBM)


def split(x):
    high = x.astype(jnp.bfloat16)
    rest = x - high.astype(jnp.float32)
    mid = rest.astype(jnp.bfloat16)
    low = (rest - mid.astype(jnp.float32)).astype(jnp.bfloat16)
    return high, mid, low


def streamed_dot(left, merged):
    high, mid, low = split(left.T)
    stack = jnp.concatenate([high, mid, low, jnp.zeros_like(low)], axis=1)
    result = jnp.dot(
        jnp.concatenate(split(merged)[:PARTS_RIGHT], axis=1),
        jnp.concatenate([stack] * PARTS_RIGHT, axis=0),
        preferred_element_type=jnp.float32,
    ).T
    return result[:RANK] + (result[RANK : 2 * RANK] + result[2 * RANK : 3 * RANK])


def turned_dot(left, merged):
    stack = jnp.concatenate(split(left), axis=0)
    result = jnp.dot(
        jnp.concatenate([stack] * PARTS_RIGHT, axis=1),
        jnp.concatenate(split(merged.T)[:PARTS_RIGHT], axis=0),
        preferred_element_type=jnp.float32,
    )
    return result[:RANK] + (result[RANK : 2 * RANK] + result[2 * RANK :])


def fetches(g_ref, e_ref, g_buf, e_refs, sems, m):
    return (
        pltpu.make_async_copy(g_ref.at[0, m], g_buf, sems.at[m, 0]),
        pltpu.make_async_copy(e_ref.at[0, m], e_refs, sems.at[m, 1]),
    )


def half_of(core, own):
    return pl.ds(pl.multiple_of((core if own else 1 - core) * HALF, HALF), HALF)


def left_kernel(
    core_ref, g_ref, e_ref, w_ref, left_ref, kept_ref, half_ref, g_buf, e_buf, w_buf, sems, w_sem
):
    w_copy = pltpu.make_async_copy(w_ref, w_buf, w_sem)
    w_copy.start()
    held = [kept_ref.at[m] if m < KEPT else e_buf.at[m - KEPT] for m in range(MATS)]
    copies = [
        fetches(g_ref, e_ref, g_buf.at[m], held[m], sems, m) for m in range(MATS)
    ]
    for pair in copies:
        for copy in pair:
            copy.start()
    w_copy.wait()
    for m in range(MATS):
        stack = jnp.concatenate(split(w_buf[m]), axis=0)
        for copy in copies[m]:
            copy.wait()
        merged = g_buf[m].astype(jnp.float32) + held[m][...]
        if m < KEPT:
            kept_ref[m] = merged
        else:
            first = core_ref[0] == 0
            half_ref[m - KEPT] = jnp.where(first, merged[HALF:], merged[:HALF])
        total = jnp.dot(
            jnp.concatenate([stack] * PARTS_LEFT, axis=1),
            jnp.concatenate(split(merged)[:PARTS_LEFT], axis=0),
            preferred_element_type=jnp.float32,
        )
        left_ref[:, 0, at(m)] = total[:RANK] + (total[RANK : 2 * RANK] + total[2 * RANK :])


def local_left(core, gradients, error_feedback, warm_rows):
    return pl.pallas_call(
        left_kernel,
        in_specs=[pl.BlockSpec(memory_space=pltpu.SMEM)] + [ANYWHERE] * 3,
        out_specs=[WHOLE] * 3,
        out_shape=[
            pltpu.VMEM((RANK, 1, WIDTH), jnp.float32),
            pltpu.VMEM((KEPT, ROWS, HALF), jnp.float32),
            pltpu.VMEM((MATS - KEPT, HALF, HALF), jnp.float32),
        ],
        scratch_shapes=[
            pltpu.VMEM((MATS, ROWS, HALF), jnp.bfloat16),
            pltpu.VMEM((MATS - KEPT, ROWS, HALF), jnp.float32),
            pltpu.VMEM((MATS, RANK, ROWS), jnp.float32),
            pltpu.SemaphoreType.DMA((MATS, 2)),
            pltpu.SemaphoreType.DMA,
        ],
        compiler_params=PARAMS,
        name="local_left",
    )(core, in_hbm(gradients), in_hbm(error_feedback), in_hbm(warm_rows))


def right_other_kernel(core_ref, kept_ref, half_ref, left_ref, out_ref, gram_ref):
    rows = half_of(core_ref[0], False)
    for m in range(MATS):
        left = left_ref[:, 0, at(m)]
        gram = lax.dot_general(
            left,
            left,
            (((1,), (1,)), ((), ())),
            precision=EXACT,
            preferred_element_type=jnp.float32,
        )
        gram = jnp.concatenate(
            [gram, jnp.zeros((RANK, 128 - RANK), jnp.float32)], axis=1
        )
        gram_ref[:, 0, m * 128 : (m + 1) * 128] = gram
        out_ref[:, 0, WIDTH + m * 128 : WIDTH + (m + 1) * 128] = gram
        merged = kept_ref[m, rows, :] if m < KEPT else half_ref[m - KEPT]
        out_ref[:, 0, at(m)] = streamed_dot(left, merged)


def right_own_kernel(
    core_ref, kept_ref, g_ref, e_ref, left_ref, out_ref, g_buf, e_buf, sems
):
    rows = half_of(core_ref[0], True)
    copies = {}
    for m in range(KEPT, MATS):
        copies[m] = (
            pltpu.make_async_copy(g_ref.at[0, m, rows], g_buf.at[m - KEPT], sems.at[m, 0]),
            pltpu.make_async_copy(e_ref.at[0, m, rows], e_buf.at[m - KEPT], sems.at[m, 1]),
        )
        for copy in copies[m]:
            copy.start()
    for m in range(MATS):
        if m < KEPT:
            merged = kept_ref[m, rows, :]
        else:
            for copy in copies[m]:
                copy.wait()
            merged = g_buf[m - KEPT].astype(jnp.float32) + e_buf[m - KEPT]
        out_ref[:, 0, at(m)] = turned_dot(left_ref[:, 0, at(m)], merged)


def right_other(core, kept, half, left):
    return pl.pallas_call(
        right_other_kernel,
        in_specs=[pl.BlockSpec(memory_space=pltpu.SMEM)] + [WHOLE] * 3,
        out_specs=[WHOLE] * 2,
        out_shape=[
            pltpu.VMEM((RANK, 1, WIDTH + MATS * 128), jnp.float32),
            pltpu.VMEM((RANK, 1, MATS * 128), jnp.float32),
        ],
        compiler_params=PARAMS,
        name="right_other",
    )(core, kept, half, left)


def right_own(core, kept, gradients, error_feedback, left):
    return pl.pallas_call(
        right_own_kernel,
        in_specs=[
            pl.BlockSpec(memory_space=pltpu.SMEM),
            WHOLE,
            ANYWHERE,
            ANYWHERE,
            WHOLE,
        ],
        out_specs=WHOLE,
        out_shape=pltpu.VMEM((RANK, 1, WIDTH), jnp.float32),
        scratch_shapes=[
            pltpu.VMEM((MATS - KEPT, HALF, HALF), jnp.bfloat16),
            pltpu.VMEM((MATS - KEPT, HALF, HALF), jnp.float32),
            pltpu.SemaphoreType.DMA((MATS, 2)),
        ],
        compiler_params=PARAMS,
        cost_estimate=pl.CostEstimate(
            flops=200_000_000, bytes_accessed=2_000_000, transcendentals=0
        ),
        name="right_own",
    )(core, kept, in_hbm(gradients), in_hbm(error_feedback), left)


def inverse_kernel(gram_ref, left_ref, inverse_ref, bases_ref):
    group, blocks = 4, RANK // 8
    wide = (8, 2 * RANK)
    row = lax.broadcasted_iota(jnp.int32, (RANK, RANK), 0)
    lane = lax.broadcasted_iota(jnp.int32, (RANK, RANK), 1)
    one = (lane == row).astype(jnp.float32)
    below = lax.broadcasted_iota(jnp.int32, wide, 0)
    tables, pivots = [], []
    for m in range(MATS):
        table = jnp.concatenate([gram_ref[:, 0, m * 128 : m * 128 + RANK], one], axis=1)
        tables.append([table[8 * b : 8 * b + 8] for b in range(blocks)])
        pivots.append([jnp.zeros(wide, jnp.float32)] * blocks)
    for j in range(0, RANK, group):
        home, top = j // 8, j % 8
        live = range(home, blocks)
        for m in range(MATS):
            table = tables[m]
            columns = [
                {b: jnp.broadcast_to(table[b][:, j + q : j + q + 1], wide) for b in live}
                for q in range(group)
            ]
            rows = [table[home][top + q : top + q + 1] for q in range(group)]
            for q in range(group):
                pivot = columns[q][home][top + q : top + q + 1]
                pivots[m][home] = jnp.where(below == top + q, pivot, pivots[m][home])
                over = 1.0 / pivot
                scaled = rows[q] * over
                factor = dict(columns[q])
                factor[home] = jnp.where(below > top + q, factor[home], 0.0)
                for later in range(q + 1, group):
                    ratio = columns[later][home][top + q : top + q + 1] * over
                    for b in live:
                        columns[later][b] = columns[later][b] - factor[b] * ratio
                    rows[later] = (
                        rows[later] - factor[home][top + later : top + later + 1] * scaled
                    )
                for b in live:
                    table[b] = table[b] - factor[b] * scaled
    for m in range(MATS):
        table = jnp.concatenate([block[:, RANK:] for block in tables[m]], axis=0)
        pivot = jnp.concatenate([block[:, RANK:] for block in pivots[m]], axis=0)
        inverse = table * lax.rsqrt(pivot)
        inverse_ref[m] = inverse
        basis = jnp.dot(
            inverse,
            left_ref[:, 0, at(m)],
            precision=EXACT,
            preferred_element_type=jnp.float32,
        )
        high, mid, _ = split(basis)
        bases_ref[m] = jnp.concatenate([high, mid, high], axis=0)


def inverse_factor(gram, left):
    return pl.pallas_call(
        inverse_kernel,
        in_specs=[WHOLE] * 2,
        out_specs=[WHOLE] * 2,
        out_shape=[
            jax.ShapeDtypeStruct((MATS, RANK, RANK), jnp.float32),
            jax.ShapeDtypeStruct((MATS, 3 * RANK, HALF), jnp.bfloat16),
        ],
        compiler_params=PARAMS,
        cost_estimate=pl.CostEstimate(
            flops=4_000_000, bytes_accessed=100_000, transcendentals=0
        ),
        name="inverse_factor",
    )(gram, left)


def finish_kernel(
    replicas,
    core_ref,
    kept_ref,
    half_ref,
    g_ref,
    e_ref,
    own_ref,
    other_ref,
    inverse_ref,
    bases_ref,
    weights_ref,
    error_ref,
    new_ref,
    right_ref,
    g_buf,
    m_buf,
    w_buf,
    e_buf,
    r_buf,
    in_sems,
    w_sems,
    out_sems,
):
    first = core_ref[0] == 0
    loads = []
    for m in range(MATS):
        pair = ()
        if m >= KEPT:
            rows = half_of(core_ref[0], True)
            pair = (
                pltpu.make_async_copy(g_ref.at[0, m, rows], g_buf.at[m - KEPT], in_sems.at[m, 0]),
                pltpu.make_async_copy(e_ref.at[0, m, rows], m_buf.at[m - KEPT], in_sems.at[m, 1]),
            )
        loads.append(
            (pltpu.make_async_copy(weights_ref.at[m], w_buf.at[m], w_sems.at[m]), *pair)
        )
    for group in loads:
        for copy in group:
            copy.start()
    stores = []

    def store(source, target):
        copy = pltpu.make_async_copy(source, target, out_sems.at[len(stores)])
        copy.start()
        stores.append(copy)

    for m in ORDER:
        own, other = own_ref[:, 0, at(m)], other_ref[:, 0, at(m)]
        total = jnp.concatenate(
            [jnp.where(first, own, other), jnp.where(first, other, own)], axis=1
        )
        inverse = inverse_ref[m]
        right = jnp.dot(
            inverse, total, precision=EXACT, preferred_element_type=jnp.float32
        ) * (1.0 / replicas)
        r_buf[m] = right
        high, mid, _ = split(right)
        rights = jnp.concatenate([high, high, mid], axis=0)
        for copy in loads[m][1:]:
            copy.wait()
        for c in range(ROWS // CHUNK):
            rows = pl.ds(c * CHUNK, CHUNK)
            update = lax.dot_general(
                rights[:, c * CHUNK : (c + 1) * CHUNK],
                bases_ref[m],
                (((0,), (0,)), ((), ())),
                preferred_element_type=jnp.float32,
            )
            if m < KEPT:
                merged = kept_ref[m, rows, :]
            else:
                fetched = g_buf[m - KEPT].astype(jnp.float32) + m_buf[m - KEPT]
                merged = jnp.where(core_ref[0] == c, fetched, half_ref[m - KEPT])
            e_buf[m, rows, :] = merged - update
            store(e_buf.at[m, rows], error_ref.at[0, m, rows])
            if c == 0:
                loads[m][0].wait()
            weights = w_buf[m, rows, :].astype(jnp.float32)
            w_buf[m, rows, :] = (weights - 0.5 * update).astype(jnp.bfloat16)
            store(w_buf.at[m, rows], new_ref.at[m, rows])
        store(r_buf.at[m], right_ref.at[m])
    for copy in stores:
        copy.wait()


def finish(
    core, kept, half, gradients, error_feedback, own, other, inverse, bases, weights, replicas
):
    def kernel(*refs):
        finish_kernel(replicas, *refs)

    return pl.pallas_call(
        kernel,
        in_specs=[
            pl.BlockSpec(memory_space=pltpu.SMEM),
            WHOLE,
            WHOLE,
            ANYWHERE,
            ANYWHERE,
            WHOLE,
            WHOLE,
            WHOLE,
            WHOLE,
            ANYWHERE,
        ],
        out_specs=[ANYWHERE] * 3,
        out_shape=[
            pltpu.HBM((1, MATS, ROWS, HALF), jnp.float32),
            pltpu.HBM((MATS, ROWS, HALF), jnp.bfloat16),
            pltpu.HBM((MATS, RANK, ROWS), jnp.float32),
        ],
        scratch_shapes=[
            pltpu.VMEM((MATS - KEPT, HALF, HALF), jnp.bfloat16),
            pltpu.VMEM((MATS - KEPT, HALF, HALF), jnp.float32),
            pltpu.VMEM((MATS, ROWS, HALF), jnp.bfloat16),
            pltpu.VMEM((MATS, ROWS, HALF), jnp.float32),
            pltpu.VMEM((MATS, RANK, ROWS), jnp.float32),
            pltpu.SemaphoreType.DMA((MATS, 2)),
            pltpu.SemaphoreType.DMA((MATS,)),
            pltpu.SemaphoreType.DMA((MATS * (1 + 2 * ROWS // CHUNK),)),
        ],
        compiler_params=PARAMS,
        name="finish",
    )(
        core,
        kept,
        half,
        in_hbm(gradients),
        in_hbm(error_feedback),
        own,
        other,
        inverse,
        bases,
        in_hbm(weights),
    )


def exchange(blocks):
    return lax.all_to_all(blocks, "dp", 0, 0, axis_index_groups=LAYERS, tiled=True)


def sum_over_replicas(blocks, beside=None):
    part = jnp.sum(exchange(blocks), axis=0)
    result = None
    if beside is not None:
        work, value = beside
        part, value = lax.optimization_barrier((part, value))
    met = []
    for meeting in MEETINGS:
        partners = [
            ((y * Z + z) * X + x, (y * Z + meeting[z]) * X + x)
            for y in range(Y)
            for z in range(Z)
            for x in range(X)
        ]
        met.append(lax.ppermute(part, "dp", partners))
    if beside is not None:
        result = work(value)
        met, result = lax.optimization_barrier((met, result))
    total = (part + met[0]) + (met[1] + met[2])
    return exchange(jnp.broadcast_to(total[None], blocks.shape)), result


def body(gradients, error_feedback, warm_start, weights):
    replicas = lax.axis_size("dp")
    core = lax.axis_index("tensor").astype(jnp.int32)[None]
    with jax.named_scope("left"):
        blocks, kept, half = local_left(
            core, gradients, error_feedback, jnp.swapaxes(warm_start, 1, 2)
        )
    with jax.named_scope("sum_left"):
        blocks, core = lax.optimization_barrier((blocks, core))
        left, _ = sum_over_replicas(blocks)
    with jax.named_scope("right"):
        other, gram = right_other(core, kept, half, left)
        received = lax.ppermute(other, "tensor", PAIR)
        own = right_own(core, kept, gradients, error_feedback, left)
        own, gram = lax.optimization_barrier(
            (own + received[:, :, :WIDTH], gram + received[:, :, WIDTH:])
        )
    with jax.named_scope("sum_right"):
        own, (inverse, bases) = sum_over_replicas(own, (lambda pair: inverse_factor(*pair), (gram, left)))
        other = lax.ppermute(own, "tensor", PAIR)
    with jax.named_scope("finish"):
        next_error, new_weights, right_rows = finish(
            core,
            kept,
            half,
            gradients,
            error_feedback,
            own,
            other,
            inverse,
            bases,
            weights,
            replicas,
        )
    return (next_error, new_weights, jnp.swapaxes(right_rows, 1, 2))


def solution(mesh):
    return jax.shard_map(
        body,
        mesh=mesh,
        in_specs=(
            P("dp", None, None, "tensor"),
            P("dp", None, None, "tensor"),
            P(),
            P(None, None, "tensor"),
        ),
        out_specs=(P("dp", None, None, "tensor"), P(None, None, "tensor"), P()),
        check_vma=False,
    )
```
